512 devices in a mesh: grp: 16 (over y_hi, x, core), dev: 32 (over y_lo, z).
Axes of the slice: x: 4, y: 4 (y_hi: 2, y_lo: 2; y = y_hi * 2 + y_lo), z: 16, core: 2. Of those that a mesh axis runs over, the one named last changes fastest.
Arguments:
- ctx_hidden: bfloat16 [2048, 3584], P('dev'), may hold values from -410 to 410
- step_hidden: bfloat16 [1536, 64, 3584], P(('grp', 'dev')), may hold values from -410 to 410
- norm_gain: float32 [3584], replicated, may hold values from 0.1 to 1.9
- w_query: bfloat16 [3584, 1792], P('dev'), may hold values from -4 to 4
- w_keyval: bfloat16 [3584, 512], P('dev'), may hold values from -24 to 24
- step_lengths: int32 [1536], P(('grp', 'dev')), may hold values from 1 to 64, as said below
- step_mask: int32 [1536, 64, 64], P(('grp', 'dev')), may hold values 0 or 1
Outputs:
- attn_out: bfloat16 [1536, 64, 1792], P(('grp', 'dev'))
The draws below stay inside these ranges and needn't reach their ends.
Inputs may be any that keep to these rules, and one draw needn't show every extreme that they name: `step_lengths`: each step's live tokens stand at its front; some solution fills all 64 slots.
All inputs are finite; a program needn't handle non-finite values. No bound on the sum of `step_mask` on one device may be relied on, other than what follows from the above.
Results may differ from the reference program's by a relative error of at most 0.009.
The reference program's roundings to bfloat16 on the way count: a program that leaves them out, or rounds other values in their place, can miss the bound.
Values may be sent and summed in bfloat16 or wider, within the bound.
No kernel may reach another device: no remote copies, remote signals or barrier semaphores. Data moves between devices by JAX's collectives and lax.ppermute only.
A program may use at most 128 MiB of HBM per device.

```python
import math
import jax
import jax.numpy as jnp
from jax import lax

MODEL_WIDTH = 3584
QUERY_HEADS = 14
KEYVAL_HEADS = 2
HEAD_SIZE = 128
STEP_SLOTS = 64
SAMPLES = 1536
CONTEXT_TOKENS = 2048


def with_scales(key, plain_rows):
    key_rows, key_cols = jax.random.split(key)
    row_scale = jnp.exp(jax.random.uniform(key_rows, (plain_rows.shape[0], 1), jnp.float32) * math.log(10.0))
    col_scale = jnp.exp(jax.random.uniform(key_cols, (1, MODEL_WIDTH), jnp.float32) * math.log(10.0))
    return plain_rows * row_scale * col_scale


def draw_ctx_hidden(key, part):
    key = jax.random.fold_in(key, 1)
    key_drawn, key_scale = jax.random.split(key)
    plain_rows = jax.random.truncated_normal(key_drawn, -4.0, 4.0, (CONTEXT_TOKENS, MODEL_WIDTH), jnp.float32)
    return with_scales(key_scale, plain_rows).astype(jnp.bfloat16)


def draw_step_hidden(key, part):
    key = jax.random.fold_in(key, 2)
    key_drawn, key_scale = jax.random.split(key)
    plain_rows = jax.random.truncated_normal(key_drawn, -4.0, 4.0, (SAMPLES * STEP_SLOTS, MODEL_WIDTH), jnp.float32)
    drawn_rows = with_scales(key_scale, plain_rows).reshape(SAMPLES, STEP_SLOTS, MODEL_WIDTH)
    return drawn_rows.astype(jnp.bfloat16)


def draw_w_query(key, part):
    key = jax.random.fold_in(key, 3)
    score_matrix = jax.random.truncated_normal(key, -4.0, 4.0, (MODEL_WIDTH, QUERY_HEADS * HEAD_SIZE), jnp.float32) / math.sqrt(MODEL_WIDTH)
    return score_matrix.astype(jnp.bfloat16)


def draw_w_keyval(key, part):
    key = jax.random.fold_in(key, 4)
    score_matrix = jax.random.truncated_normal(key, -4.0, 4.0, (MODEL_WIDTH, 2 * KEYVAL_HEADS * HEAD_SIZE), jnp.float32) / math.sqrt(MODEL_WIDTH)
    return score_matrix.astype(jnp.bfloat16)


def draw_step_lengths(key, part):
    key = jax.random.fold_in(key, 5)
    key_draw, key_pick = jax.random.split(key)
    lengths = jax.random.randint(key_draw, (SAMPLES,), 1, STEP_SLOTS + 1, jnp.int32)
    full_index = jax.random.randint(key_pick, (), 0, SAMPLES, jnp.int32)
    return lengths.at[full_index].set(STEP_SLOTS)


def place_ends(values, own_key, smallest, top_value):
    place = [jax.random.randint(jax.random.fold_in(own_key, axis), (), 0, length) for axis, length in enumerate(values.shape)]
    main_axis = values.shape.index(max(values.shape))
    neighbour = place[:main_axis] + [(place[main_axis] + 1) % values.shape[main_axis]] + place[main_axis + 1:]
    return values.at[tuple(place)].set(smallest).at[tuple(neighbour)].set(top_value)


def setup_inputs(seed: int = 0) -> dict:
    key_list = jax.random.split(jax.random.key(seed), 8)
    ctx_hidden = draw_ctx_hidden(jax.random.fold_in(key_list[7], 71), 0)
    step_hidden = draw_step_hidden(jax.random.fold_in(key_list[7], 71), 0)
    norm_gain = jnp.clip(1.0 + 0.18 * jax.random.normal(key_list[2], (MODEL_WIDTH,), jnp.float32), 0.1, 1.9)
    w_query = draw_w_query(jax.random.fold_in(key_list[7], 71), 0)
    w_keyval = draw_w_keyval(jax.random.fold_in(key_list[7], 71), 0)
    step_lengths = draw_step_lengths(jax.random.fold_in(key_list[7], 71), 0)
    step_mask = place_ends((jax.random.randint(key_list[6], (SAMPLES, STEP_SLOTS, STEP_SLOTS), 0, 4) < 3).astype(jnp.int32), jax.random.fold_in(key_list[6], 1), 0, 1)
    return dict(ctx_hidden=ctx_hidden, step_hidden=step_hidden, norm_gain=norm_gain, w_query=w_query, w_keyval=w_keyval, step_lengths=step_lengths, step_mask=step_mask)


NEG_FILL = -1e+30

def rms_norm(hidden_rows, norm_gain):
    widened = hidden_rows.astype(jnp.float32)
    inverse = lax.rsqrt(lax.optimization_barrier(jnp.mean(widened * widened, axis=-1, keepdims=True)) + 1e-06)
    return (widened * inverse * norm_gain).astype(jnp.bfloat16)

def rounded(values):
    return lax.optimization_barrier(values.astype(jnp.bfloat16))

def reference(ctx_hidden, step_hidden, norm_gain, w_query, w_keyval, step_lengths, step_mask):
    head_groups = QUERY_HEADS // KEYVAL_HEADS
    score_scale = 1.0 / math.sqrt(HEAD_SIZE)
    normed_context = rms_norm(ctx_hidden, norm_gain)
    problem_keyval = rounded(jnp.dot(normed_context, w_keyval, preferred_element_type=jnp.float32))
    problem_keyval = problem_keyval.astype(jnp.float32).reshape(CONTEXT_TOKENS, 2, KEYVAL_HEADS, HEAD_SIZE)
    context_keys = problem_keyval[:, 0]
    context_values = problem_keyval[:, 1]
    positions = jnp.arange(STEP_SLOTS, dtype=jnp.int32)
    causal = positions[None, :] <= positions[:, None]
    diagonal = positions[None, :] == positions[:, None]
    block_extent = 4

    def one_block(inputs):
        hidden_block, length_block, mask_block = inputs
        normed_step = rms_norm(hidden_block.reshape(block_extent * STEP_SLOTS, MODEL_WIDTH), norm_gain)
        query_block = rounded(jnp.dot(normed_step, w_query, preferred_element_type=jnp.float32))
        query_block = query_block.astype(jnp.float32).reshape(block_extent, STEP_SLOTS, KEYVAL_HEADS, head_groups, HEAD_SIZE)
        solution_keyval = rounded(jnp.dot(normed_step, w_keyval, preferred_element_type=jnp.float32))
        solution_keyval = solution_keyval.astype(jnp.float32).reshape(block_extent, STEP_SLOTS, 2, KEYVAL_HEADS, HEAD_SIZE)
        step_keys = solution_keyval[:, :, 0]
        step_values = solution_keyval[:, :, 1]
        ctx_scores = jnp.einsum('bthgd,nhd->bthgn', query_block, context_keys) * score_scale
        step_scores = jnp.einsum('bthgd,buhd->bthgu', query_block, step_keys) * score_scale
        allowed = causal[None] & (diagonal[None] | (mask_block == 1)) & (positions[None, None, :] < length_block[:, None, None])
        step_scores = jnp.where(allowed[:, :, None, None, :], step_scores, NEG_FILL)
        row_top = jnp.maximum(ctx_scores.max(-1), step_scores.max(-1))
        ctx_weights = jnp.exp(ctx_scores - row_top[..., None])
        step_weights = jnp.exp(step_scores - row_top[..., None])
        weight_sum = ctx_weights.sum(-1) + step_weights.sum(-1)
        attended = jnp.einsum('bthgn,nhd->bthgd', rounded(ctx_weights).astype(jnp.float32), context_values)
        attended = attended + jnp.einsum('bthgu,buhd->bthgd', rounded(step_weights).astype(jnp.float32), step_values)
        attended = attended / weight_sum[..., None]
        live_rows = positions[None, :] < length_block[:, None]
        attended = jnp.where(live_rows[:, :, None, None, None], attended, 0.0)
        return attended.reshape(block_extent, STEP_SLOTS, QUERY_HEADS * HEAD_SIZE).astype(jnp.bfloat16)
    blocks = SAMPLES // block_extent
    result = lax.map(one_block, (step_hidden.reshape(blocks, block_extent, STEP_SLOTS, MODEL_WIDTH), step_lengths.reshape(blocks, block_extent), step_mask.reshape(blocks, block_extent, STEP_SLOTS, STEP_SLOTS)))
    return result.reshape(SAMPLES, STEP_SLOTS, QUERY_HEADS * HEAD_SIZE)
```

```python
import functools
import math

import jax
import jax.numpy as jnp
from jax import lax
from jax.experimental import pallas as pl
from jax.experimental.pallas import tpu as pltpu
from jax.sharding import Mesh
from jax.sharding import PartitionSpec as P

HEAD_SIZE = 128
NEG_FILL = -1e30
AXES = ("yh", "x", "core", "yl", "z")
SWAP = [(0, 1), (1, 0)]


def rms_norm(hidden_rows, norm_gain):
    widened = hidden_rows.astype(jnp.float32)
    inverse = lax.rsqrt(jnp.mean(widened * widened, axis=-1, keepdims=True) + 1e-06)
    return (widened * inverse * norm_gain).astype(jnp.bfloat16)


def dot(a, b):
    return jnp.dot(a, b, preferred_element_type=jnp.float32)


def spread(block, axis):
    size = lax.axis_size(axis)
    return lax.all_to_all(jnp.broadcast_to(block[None], (size,) + block.shape), axis, 0, 0, tiled=True)


def attend_kernel(heads, query, keys, values, step_keys, step_values, allowed, out):
    slots = query.shape[0]
    scale = math.log2(math.e) / math.sqrt(HEAD_SIZE)
    rows = jnp.concatenate([query[:, h * HEAD_SIZE : (h + 1) * HEAD_SIZE] for h in range(heads)], 0)
    contract = (((1,), (1,)), ((), ()))
    far = lax.dot_general(rows, keys[...], contract, preferred_element_type=jnp.float32)
    near = lax.dot_general(rows, step_keys[...], contract, preferred_element_type=jnp.float32)
    seen = jnp.concatenate([allowed[...][:, :slots].astype(jnp.float32)] * heads, 0) > 0.5
    near = jnp.where(seen, near, NEG_FILL)
    top = jnp.maximum(far.max(-1, keepdims=True), near.max(-1, keepdims=True))
    far_weights = jnp.exp2((far - top) * scale)
    near_weights = jnp.exp2((near - top) * scale)
    total = far_weights.sum(-1, keepdims=True) + near_weights.sum(-1, keepdims=True)
    attended = dot(far_weights.astype(jnp.bfloat16), values[...])
    attended = attended + dot(near_weights.astype(jnp.bfloat16), step_values[...])
    attended = (attended / total).astype(jnp.bfloat16)
    out[...] = jnp.concatenate([attended[h * slots : (h + 1) * slots] for h in range(heads)], 1)


def attend(query, keys, values, step_keyval, allowed, slots):
    rows, cols = query.shape
    heads = cols // HEAD_SIZE
    tokens = keys.shape[0]
    whole = pl.BlockSpec((tokens, HEAD_SIZE), lambda i: (0, 0))
    return pl.pallas_call(
        functools.partial(attend_kernel, heads),
        grid=(rows // slots,),
        in_specs=[
            pl.BlockSpec((slots, cols), lambda i: (i, 0)),
            whole,
            whole,
            pl.BlockSpec((slots, HEAD_SIZE), lambda i: (i, 0)),
            pl.BlockSpec((slots, HEAD_SIZE), lambda i: (i, 1)),
            pl.BlockSpec((slots, allowed.shape[1]), lambda i: (i, 0)),
        ],
        out_specs=pl.BlockSpec((slots, cols), lambda i: (i, 0)),
        out_shape=jax.ShapeDtypeStruct((rows, cols), jnp.bfloat16),
        compiler_params=pltpu.CompilerParams(vmem_limit_bytes=40 * 2**20),
        cost_estimate=pl.CostEstimate(
            flops=4 * rows * cols * tokens, bytes_accessed=4 * rows * cols, transcendentals=rows * heads * tokens
        ),
    )(query, keys, values, step_keyval, step_keyval, allowed)


def local(ctx_hidden, step_hidden, norm_gain, w_query, w_keyval, step_lengths, step_mask):
    samples, slots, features = step_hidden.shape
    rows = samples * slots
    kv_heads = w_keyval.shape[1] // (2 * HEAD_SIZE)
    cols = w_query.shape[1] // kv_heads
    share = w_query.shape[0]
    core, x = lax.axis_index("core"), lax.axis_index("x")

    own_query = lax.dynamic_slice_in_dim(w_query, core * cols, cols, 1)
    pair_query = lax.all_gather(own_query, "yl", axis=0, tiled=True)
    full_query = lax.all_gather(pair_query, "z", axis=0, tiled=True)

    own_kv = lax.dynamic_slice_in_dim(w_keyval, ((x % 2) * kv_heads + core) * HEAD_SIZE, HEAD_SIZE, 1)
    pair_kv = lax.all_gather(own_kv, "yl", axis=0, tiled=True)
    half_kv = spread(pair_kv, "z").reshape(features, HEAD_SIZE)
    other_kv = lax.ppermute(half_kv, "x", [(i, i ^ 1) for i in range(lax.axis_size("x"))])

    def reorder(normed):
        count = normed.shape[0]
        return normed.reshape(count, 2, features // share // 2, share).swapaxes(1, 2).reshape(count, features)

    token_share = ctx_hidden.shape[0] // 2
    own_context = lax.dynamic_slice_in_dim(ctx_hidden, (x // 2) * token_share, token_share, 0)
    normed_context = reorder(rms_norm(own_context, norm_gain))
    context_block = dot(normed_context, half_kv).astype(jnp.bfloat16)
    context_block = lax.all_gather(context_block, "yl", axis=0, tiled=True)
    context_block = spread(context_block, "z").reshape(-1, HEAD_SIZE)
    context_all = spread(context_block, "x")
    keys = jnp.concatenate([context_all[0], context_all[2]], 0)
    values = jnp.concatenate([context_all[1], context_all[3]], 0)

    positions = lax.iota(jnp.int32, slots)
    causal = positions[None, :] <= positions[:, None]
    diagonal = positions[None, :] == positions[:, None]
    allowed = (
        causal[None]
        & (diagonal[None] | (step_mask == 1))
        & (positions[None, None, :] < step_lengths[:, None, None])
    )
    allowed = jnp.pad(allowed.astype(jnp.bfloat16).reshape(rows, slots), ((0, 0), (0, HEAD_SIZE - slots)))
    normed_step = reorder(rms_norm(step_hidden.reshape(rows, features), norm_gain))
    own_rows = jnp.concatenate([normed_step, allowed], 1)
    both_rows = jnp.concatenate([own_rows, lax.ppermute(own_rows, "core", SWAP)], 0)
    normed_rows, allowed_rows = both_rows[:, :features], both_rows[:, features:]

    is_key = x % 2 == 0
    keyval_weights = jnp.concatenate(
        [jnp.where(is_key, half_kv, other_kv), jnp.where(is_key, other_kv, half_kv)], 1
    )
    step_keyval = dot(normed_rows, keyval_weights).astype(jnp.bfloat16)
    query = dot(normed_rows, full_query).astype(jnp.bfloat16)
    attended = attend(query, keys, values, step_keyval, allowed_rows, slots)

    mine, theirs = attended[:rows], lax.ppermute(attended[rows:], "core", SWAP)
    first = core == 0
    result = jnp.concatenate([jnp.where(first, mine, theirs), jnp.where(first, theirs, mine)], 1)
    result = result.reshape(samples, slots, kv_heads * cols)
    live_rows = positions[None, :] < step_lengths[:, None]
    return jnp.where(live_rows[:, :, None], result, jnp.bfloat16(0.0))


def solution(mesh):
    five = Mesh(mesh.devices.reshape(2, 4, 2, 2, 16), AXES)
    dev, everywhere = ("yl", "z"), AXES
    placed = (
        P(dev, None),
        P(everywhere, None, None),
        P(),
        P(dev, None),
        P(dev, None),
        P(everywhere),
        P(everywhere, None, None),
    )
    return jax.shard_map(
        local, mesh=five, in_specs=placed, out_specs=P(everywhere, None, None), check_vma=False
    )
```

```python
import functools
import math

import jax
import jax.numpy as jnp
from jax import lax
from jax.experimental import pallas as pl
from jax.experimental.pallas import tpu as pltpu
from jax.sharding import Mesh
from jax.sharding import PartitionSpec as P

HEAD_SIZE = 128
NEG_FILL = -1e30
AXES = ("yh", "x", "core", "yl", "z")
SWAP = [(0, 1), (1, 0)]
CHUNK = 1024
DEPTH = 256


def rms_norm(hidden_rows, norm_gain):
    widened = hidden_rows.astype(jnp.float32)
    inverse = lax.rsqrt(jnp.mean(widened * widened, axis=-1, keepdims=True) + 1e-06)
    return (widened * inverse * norm_gain).astype(jnp.bfloat16)


def dot(a, b):
    return jnp.dot(a, b, preferred_element_type=jnp.float32)


def spread(block, axis):
    size = math.prod(lax.axis_size(one) for one in (axis if isinstance(axis, tuple) else (axis,)))
    return lax.all_to_all(jnp.broadcast_to(block[None], (size,) + block.shape), axis, 0, 0, tiled=True)


def attend_sample(query, keys, values, step_keys, step_values, seen, chunk):
    scale = math.log2(math.e) / math.sqrt(HEAD_SIZE)
    contract = (((1,), (1,)), ((), ()))
    near = lax.dot_general(query, step_keys, contract, preferred_element_type=jnp.float32)
    near = jnp.where(seen, near, NEG_FILL)
    starts = range(0, keys.shape[0], chunk)
    far = [
        lax.dot_general(query, keys[at : at + chunk], contract, preferred_element_type=jnp.float32) for at in starts
    ]
    top = near.max(-1, keepdims=True)
    for scores in far:
        top = jnp.maximum(top, scores.max(-1, keepdims=True))
    top = top * scale
    weights = jnp.exp2(near * scale - top)
    total = weights.sum(-1, keepdims=True)
    attended = dot(weights.astype(jnp.bfloat16), step_values)
    for at, scores in zip(starts, far):
        weights = jnp.exp2(scores * scale - top)
        total = total + weights.sum(-1, keepdims=True)
        attended = attended + dot(weights.astype(jnp.bfloat16), values[at : at + chunk])
    return (attended / total).astype(jnp.bfloat16)


def attend_kernel(
    chunks, slots, low, high, low_weights, high_weights, context, step_keys, step_values, allowed, out, *scratch
):
    total, query, keys, values = scratch
    step = pl.program_id(0)
    heads = query.shape[1] // HEAD_SIZE

    @pl.when(step == 0)
    def _():
        total[...] = jnp.zeros_like(total)
        count, quarter = context.shape[1], HEAD_SIZE // 2
        for hi in range(context.shape[0] // 4):
            for x in range(4):
                to, lane = (keys, values)[x // 2], x % 2 * quarter
                for side in range(2):
                    at = (hi * 2 + side) * count
                    to[at : at + count, lane : lane + quarter] = context[
                        hi * 4 + x, :, side * quarter : (side + 1) * quarter
                    ]

    @pl.when(step < chunks)
    def _():
        total[...] += dot(low[...], low_weights[...]) + dot(high[...], high_weights[...])

    @pl.when(step == chunks - 1)
    def _():
        query[...] = total[...].astype(jnp.bfloat16)

    @pl.when(step >= chunks)
    def _():
        rows = out.shape[0]
        first = (step - chunks) * rows
        for at in range(0, rows, slots):
            here = slice(at, at + slots)
            own = query[pl.ds(pl.multiple_of(first + at, slots), slots), :]
            own = jnp.concatenate([own[:, h * HEAD_SIZE : (h + 1) * HEAD_SIZE] for h in range(heads)], 0)
            seen = jnp.concatenate([allowed[here, :slots].astype(jnp.float32)] * heads, 0) > 0.5
            result = attend_sample(own, keys, values, step_keys[here], step_values[here], seen, CHUNK)
            out[here, :] = jnp.concatenate([result[h * slots : (h + 1) * slots] for h in range(heads)], 1)


def attend(normed, query_weights, context, step_keyval, allowed, slots):
    rows, features = normed.shape
    half, cols = query_weights.shape[0], query_weights.shape[1] // 2
    tokens = context.shape[0] * context.shape[1] // 2
    chunks = half // DEPTH
    at_once = 2 * slots
    project_at = lambda i: jnp.minimum(i, chunks - 1)
    attend_at = lambda i: jnp.maximum(i - chunks, 0)
    return pl.pallas_call(
        functools.partial(attend_kernel, chunks, slots),
        grid=(chunks + rows // at_once,),
        in_specs=[
            pl.BlockSpec((rows, DEPTH), lambda i: (0, project_at(i))),
            pl.BlockSpec((rows, DEPTH), lambda i: (0, chunks + project_at(i))),
            pl.BlockSpec((DEPTH, cols), lambda i: (project_at(i), 0)),
            pl.BlockSpec((DEPTH, cols), lambda i: (project_at(i), 1)),
            pl.BlockSpec(context.shape, lambda i: (0, 0, 0)),
            pl.BlockSpec((at_once, HEAD_SIZE), lambda i: (attend_at(i), 0)),
            pl.BlockSpec((at_once, HEAD_SIZE), lambda i: (attend_at(i), 1)),
            pl.BlockSpec((at_once, allowed.shape[1]), lambda i: (attend_at(i), 0)),
        ],
        out_specs=pl.BlockSpec((at_once, cols), lambda i: (attend_at(i), 0)),
        out_shape=jax.ShapeDtypeStruct((rows, cols), jnp.bfloat16),
        scratch_shapes=[pltpu.VMEM((rows, cols), jnp.float32), pltpu.VMEM((rows, cols), jnp.bfloat16)]
        + [pltpu.VMEM((tokens, HEAD_SIZE), jnp.bfloat16)] * 2,
        compiler_params=pltpu.CompilerParams(vmem_limit_bytes=44 * 2**20),
        cost_estimate=pl.CostEstimate(
            flops=4 * rows * cols * tokens + 2 * rows * cols * features,
            bytes_accessed=2 * features * cols,
            transcendentals=rows * tokens * cols // HEAD_SIZE,
        ),
    )(normed, normed, query_weights, query_weights, context, step_keyval, step_keyval, allowed)


def project(rows, packed):
    features, width = rows.shape[1] // 2, packed.shape[1] // 2
    return dot(rows[:, :features], packed[:, :width]) + dot(rows[:, features:], packed[:, width:])


def pack(block):
    half = block.shape[-2] // 2
    return jnp.concatenate([block[..., :half, :], block[..., half:, :]], -1)


def local(ctx_hidden, step_hidden, norm_gain, w_query, w_keyval, step_lengths, step_mask):
    samples, slots, features = step_hidden.shape
    rows = samples * slots
    kv_heads = w_keyval.shape[1] // (2 * HEAD_SIZE)
    cols = w_query.shape[1] // kv_heads
    chips = lax.axis_size("x")
    quarter = 2 * HEAD_SIZE // chips
    core, x = lax.axis_index("core"), lax.axis_index("x")

    own_query = lax.dynamic_slice_in_dim(w_query, core * cols, cols, 1)
    start = (x // 2) * kv_heads * HEAD_SIZE + core * HEAD_SIZE + (x % 2) * quarter
    own_kv = lax.dynamic_slice_in_dim(w_keyval, start, quarter, 1)
    pair = lax.all_gather(jnp.concatenate([own_query, own_kv], 1), "yl", axis=0)
    pair_query = jnp.concatenate([pair[0, :, :cols], pair[1, :, :cols]], 1)
    pair_kv = jnp.concatenate([pair[0, :, cols:], pair[1, :, cols:]], 1)
    pair_query, pair_kv, step_hidden, ctx_hidden = lax.optimization_barrier(
        (pair_query, pair_kv, step_hidden, ctx_hidden)
    )
    query_weights = lax.all_gather(pair_query, "z", axis=0, tiled=True)
    yh = lax.axis_index("yh")
    rows_half = pair_kv.shape[0] // 2
    half_kv = spread(lax.dynamic_slice_in_dim(pair_kv, yh * rows_half, rows_half, 0), "z")
    rest_kv = lax.ppermute(half_kv, "yh", SWAP)
    low_first = yh == 0
    part_kv = jnp.concatenate([jnp.where(low_first, half_kv, rest_kv), jnp.where(low_first, rest_kv, half_kv)], 1)
    part_kv = part_kv.reshape(-1, 2 * quarter)

    own_tokens = ctx_hidden.shape[0] // 2
    own_context = lax.dynamic_slice_in_dim(ctx_hidden, yh * own_tokens, own_tokens, 0)
    context = project(rms_norm(own_context, norm_gain), part_kv).astype(jnp.bfloat16)
    context = lax.all_gather(pack(context), "yl", axis=0, tiled=True)
    context = spread(spread(context, "z").reshape(-1, 2 * quarter), ("yh", "x"))

    positions = lax.iota(jnp.int32, slots)
    causal = positions[None, :] <= positions[:, None]
    diagonal = positions[None, :] == positions[:, None]
    allowed = (
        causal[None]
        & (diagonal[None] | (step_mask == 1))
        & (positions[None, None, :] < step_lengths[:, None, None])
    )
    allowed = jnp.pad(allowed.astype(jnp.bfloat16).reshape(rows, slots), ((0, 0), (0, HEAD_SIZE - slots)))
    allowed = jnp.concatenate([allowed, lax.ppermute(allowed, "core", SWAP)], 0)
    normed_step = rms_norm(step_hidden.reshape(rows, features), norm_gain)
    both_rows = jnp.concatenate([normed_step, lax.ppermute(normed_step, "core", SWAP)], 0)

    turns = [part_kv] + [
        lax.ppermute(part_kv, "x", [(i, (i - turn) % chips) for i in range(chips)]) for turn in range(1, chips)
    ]
    kv_weights = jnp.concatenate(
        [
            jnp.concatenate([one[:, :quarter] for one in turns], 1),
            jnp.concatenate([one[:, quarter:] for one in turns], 1),
        ],
        0,
    )
    step_keyval = dot(both_rows, kv_weights).astype(jnp.bfloat16)
    step_keyval = jnp.concatenate([step_keyval, step_keyval], 1)
    step_keyval = lax.dynamic_slice_in_dim(step_keyval, (chips - x) % chips * quarter, chips * quarter, 1)
    attended = attend(both_rows, query_weights, context, step_keyval, allowed, slots)

    mine, theirs = attended[:rows], lax.ppermute(attended[rows:], "core", SWAP)
    first = core == 0
    result = jnp.concatenate([jnp.where(first, mine, theirs), jnp.where(first, theirs, mine)], 1)
    result = result.reshape(samples, slots, kv_heads * cols)
    live_rows = positions[None, :] < step_lengths[:, None]
    return jnp.where(live_rows[:, :, None], result, jnp.bfloat16(0.0))


def solution(mesh):
    five = Mesh(mesh.devices.reshape(2, 4, 2, 2, 16), AXES)
    dev, everywhere = ("yl", "z"), AXES
    placed = (
        P(dev, None),
        P(everywhere, None, None),
        P(),
        P(dev, None),
        P(dev, None),
        P(everywhere),
        P(everywhere, None, None),
    )
    return jax.shard_map(
        local, mesh=five, in_specs=placed, out_specs=P(everywhere, None, None), check_vma=False
    )
```

```python
import functools
import math

import jax
import jax.numpy as jnp
from jax import lax
from jax.experimental import pallas as pl
from jax.experimental.pallas import tpu as pltpu
from jax.sharding import Mesh
from jax.sharding import PartitionSpec as P

HEAD_SIZE = 128
NEG_FILL = -1e30
AXES = ("yh", "x", "core", "yl", "z")
SWAP = [(0, 1), (1, 0)]
CHUNK = 1024
DEPTH = 896


def rms_norm(hidden_rows, norm_gain):
    widened = hidden_rows.astype(jnp.float32)
    inverse = lax.rsqrt(jnp.mean(widened * widened, axis=-1, keepdims=True) + 1e-06)
    return (widened * inverse * norm_gain).astype(jnp.bfloat16)


def dot(a, b):
    return jnp.dot(a, b, preferred_element_type=jnp.float32)


def spread(block, axis):
    size = math.prod(lax.axis_size(one) for one in (axis if isinstance(axis, tuple) else (axis,)))
    return lax.all_to_all(jnp.broadcast_to(block[None], (size,) + block.shape), axis, 0, 0, tiled=True)


def attend_sample(query, keys, values, step_keys, step_values, seen, chunk):
    scale = math.log2(math.e) / math.sqrt(HEAD_SIZE)
    contract = (((1,), (1,)), ((), ()))
    near = lax.dot_general(query, step_keys, contract, preferred_element_type=jnp.float32)
    near = jnp.where(seen, near, NEG_FILL)
    starts = range(0, keys.shape[0], chunk)
    far = [
        lax.dot_general(query, keys[at : at + chunk], contract, preferred_element_type=jnp.float32) for at in starts
    ]
    top = near.max(-1, keepdims=True)
    for scores in far:
        top = jnp.maximum(top, scores.max(-1, keepdims=True))
    top = top * scale
    weights = jnp.exp2(near * scale - top)
    total = weights.sum(-1, keepdims=True)
    attended = dot(weights.astype(jnp.bfloat16), step_values)
    for at, scores in zip(starts, far):
        weights = jnp.exp2(scores * scale - top)
        total = total + weights.sum(-1, keepdims=True)
        attended = attended + dot(weights.astype(jnp.bfloat16), values[at : at + chunk])
    return (attended / total).astype(jnp.bfloat16)


def attend_kernel(
    chunks, slots, normed, low_weights, high_weights, context, step_keyval, allowed, own_out, other_out, *scratch
):
    total, query, keys, values = scratch
    step = pl.program_id(0)
    heads = query.shape[1] // HEAD_SIZE
    depth = low_weights.shape[0]

    def unpack():
        count, quarter = context.shape[1], HEAD_SIZE // 2
        for hi in range(context.shape[0] // 4):
            for x in range(4):
                to, lane = (keys, values)[x // 2], x % 2 * quarter
                for side in range(2):
                    at = (hi * 2 + side) * count
                    to[at : at + count, lane : lane + quarter] = context[
                        hi * 4 + x, :, side * quarter : (side + 1) * quarter
                    ]

    for chunk in range(chunks):

        @pl.when(step == chunk)
        def _():
            low = normed[:, chunk * depth : (chunk + 1) * depth]
            high = normed[:, (chunks + chunk) * depth : (chunks + chunk + 1) * depth]
            both = dot(low, low_weights[...]) + dot(high, high_weights[...])
            if chunk == 0:
                total[...] = both
                unpack()
            else:
                total[...] += both

    @pl.when(step == chunks - 1)
    def _():
        query[...] = total[...].astype(jnp.bfloat16)

    def attend_rows(first, out):
        for at in range(0, out.shape[0], slots):
            here = slice(first + at, first + at + slots)
            own = query[here, :]
            own = jnp.concatenate([own[:, h * HEAD_SIZE : (h + 1) * HEAD_SIZE] for h in range(heads)], 0)
            seen = jnp.concatenate([allowed[here, :slots].astype(jnp.float32)] * heads, 0) > 0.5
            step_keys, step_values = step_keyval[here, :HEAD_SIZE], step_keyval[here, HEAD_SIZE:]
            result = attend_sample(own, keys, values, step_keys, step_values, seen, CHUNK)
            out[at : at + slots, :] = jnp.concatenate(
                [result[h * slots : (h + 1) * slots] for h in range(heads)], 1
            )

    @pl.when(step == chunks)
    def _():
        attend_rows(0, own_out)

    @pl.when(step == chunks + 1)
    def _():
        attend_rows(own_out.shape[0], other_out)


def attend(normed, query_weights, context, step_keyval, allowed, slots):
    rows, features = normed.shape
    half, cols = query_weights.shape[0], query_weights.shape[1] // 2
    tokens = context.shape[0] * context.shape[1] // 2
    chunks = half // DEPTH
    here = pl.BlockSpec(memory_space=pltpu.VMEM)
    return pl.pallas_call(
        functools.partial(attend_kernel, chunks, slots),
        grid=(chunks + 2,),
        in_specs=[
            here,
            pl.BlockSpec((DEPTH, cols), lambda i: (jnp.minimum(i, chunks - 1), 0)),
            pl.BlockSpec((DEPTH, cols), lambda i: (jnp.minimum(i, chunks - 1), 1)),
            here,
            pl.BlockSpec(step_keyval.shape, lambda i: (0, 0)),
            pl.BlockSpec(allowed.shape, lambda i: (0, 0)),
        ],
        out_specs=[here, here],
        out_shape=[jax.ShapeDtypeStruct((rows // 2, cols), jnp.bfloat16)] * 2,
        scratch_shapes=[pltpu.VMEM((rows, cols), jnp.float32), pltpu.VMEM((rows, cols), jnp.bfloat16)]
        + [pltpu.VMEM((tokens, HEAD_SIZE), jnp.bfloat16)] * 2,
        compiler_params=pltpu.CompilerParams(vmem_limit_bytes=44 * 2**20),
        cost_estimate=pl.CostEstimate(
            flops=4 * rows * cols * tokens + 2 * rows * cols * features,
            bytes_accessed=2 * features * cols,
            transcendentals=rows * tokens * cols // HEAD_SIZE,
        ),
    )(normed, query_weights, query_weights, context, step_keyval, allowed)


def project(rows, packed):
    features, width = rows.shape[1] // 2, packed.shape[1] // 2
    return dot(rows[:, :features], packed[:, :width]) + dot(rows[:, features:], packed[:, width:])


def pack(block):
    half = block.shape[-2] // 2
    return jnp.concatenate([block[..., :half, :], block[..., half:, :]], -1)


def local(ctx_hidden, step_hidden, norm_gain, w_query, w_keyval, step_lengths, step_mask):
    samples, slots, features = step_hidden.shape
    rows = samples * slots
    kv_heads = w_keyval.shape[1] // (2 * HEAD_SIZE)
    cols = w_query.shape[1] // kv_heads
    chips = lax.axis_size("x")
    quarter = 2 * HEAD_SIZE // chips
    core, x = lax.axis_index("core"), lax.axis_index("x")

    own_query = lax.dynamic_slice_in_dim(w_query, core * cols, cols, 1)
    start = (x // 2) * kv_heads * HEAD_SIZE + core * HEAD_SIZE + (x % 2) * quarter
    own_kv = lax.dynamic_slice_in_dim(w_keyval, start, quarter, 1)
    pair = lax.all_gather(jnp.concatenate([own_query, own_kv], 1), "yl", axis=0)
    pair_query = jnp.concatenate([pair[0, :, :cols], pair[1, :, :cols]], 1)
    pair_kv = jnp.concatenate([pair[0, :, cols:], pair[1, :, cols:]], 1)
    pair_query, pair_kv, step_hidden, ctx_hidden = lax.optimization_barrier(
        (pair_query, pair_kv, step_hidden, ctx_hidden)
    )
    query_weights = lax.all_gather(pair_query, "z", axis=0, tiled=True)
    yh = lax.axis_index("yh")
    rows_half = pair_kv.shape[0] // 2
    half_kv = spread(lax.dynamic_slice_in_dim(pair_kv, yh * rows_half, rows_half, 0), "z")
    rest_kv = lax.ppermute(half_kv, "yh", SWAP)
    low_first = yh == 0
    part_kv = jnp.concatenate([jnp.where(low_first, half_kv, rest_kv), jnp.where(low_first, rest_kv, half_kv)], 1)
    part_kv = part_kv.reshape(-1, 2 * quarter)

    own_tokens = ctx_hidden.shape[0] // 2
    own_context = lax.dynamic_slice_in_dim(ctx_hidden, yh * own_tokens, own_tokens, 0)
    context = project(rms_norm(own_context, norm_gain), part_kv).astype(jnp.bfloat16)
    context = lax.all_gather(pack(context), "yl", axis=0, tiled=True)
    part_kv = lax.optimization_barrier((part_kv, context))[0]
    context = spread(spread(context, "z").reshape(-1, 2 * quarter), ("yh", "x"))

    positions = lax.iota(jnp.int32, slots)
    causal = positions[None, :] <= positions[:, None]
    diagonal = positions[None, :] == positions[:, None]
    allowed = (
        causal[None]
        & (diagonal[None] | (step_mask == 1))
        & (positions[None, None, :] < step_lengths[:, None, None])
    )
    allowed = jnp.pad(allowed.astype(jnp.bfloat16).reshape(rows, slots), ((0, 0), (0, HEAD_SIZE - slots)))
    allowed = jnp.concatenate([allowed, lax.ppermute(allowed, "core", SWAP)], 0)
    normed_step = rms_norm(step_hidden.reshape(rows, features), norm_gain)
    both_rows = jnp.concatenate([normed_step, lax.ppermute(normed_step, "core", SWAP)], 0)

    turns = [part_kv] + [
        lax.ppermute(part_kv, "x", [(i, (i - turn) % chips) for i in range(chips)]) for turn in range(1, chips)
    ]
    kv_weights = jnp.concatenate(
        [
            jnp.concatenate([one[:, :quarter] for one in turns], 1),
            jnp.concatenate([one[:, quarter:] for one in turns], 1),
        ],
        0,
    )
    step_keyval = dot(both_rows, kv_weights).astype(jnp.bfloat16)
    step_keyval = jnp.concatenate([step_keyval, step_keyval], 1)
    step_keyval = lax.dynamic_slice_in_dim(step_keyval, (chips - x) % chips * quarter, chips * quarter, 1)
    mine, theirs = attend(both_rows, query_weights, context, step_keyval, allowed, slots)

    theirs = lax.ppermute(theirs, "core", SWAP)
    live_rows = (positions[None, :] < step_lengths[:, None]).reshape(rows, 1)
    first = core == 0
    low = jnp.where(live_rows, jnp.where(first, mine, theirs), jnp.bfloat16(0.0))
    high = jnp.where(live_rows, jnp.where(first, theirs, mine), jnp.bfloat16(0.0))
    return jnp.concatenate([low, high], 1).reshape(samples, slots, kv_heads * cols)


def solution(mesh):
    five = Mesh(mesh.devices.reshape(2, 4, 2, 2, 16), AXES)
    dev, everywhere = ("yl", "z"), AXES
    placed = (
        P(dev, None),
        P(everywhere, None, None),
        P(),
        P(dev, None),
        P(dev, None),
        P(everywhere),
        P(everywhere, None, None),
    )
    return jax.shard_map(
        local, mesh=five, in_specs=placed, out_specs=P(everywhere, None, None), check_vma=False
    )
```

```python
import functools
import math

import jax
import jax.numpy as jnp
from jax import lax
from jax.experimental import pallas as pl
from jax.experimental.pallas import tpu as pltpu
from jax.sharding import Mesh
from jax.sharding import PartitionSpec as P

HEAD_SIZE = 128
NEG_FILL = -1e30
AXES = ("yh", "x", "core", "yl", "z")
SWAP = [(0, 1), (1, 0)]
CHUNK = 1024
DEPTH = 896


def rms_norm(hidden_rows, norm_gain):
    widened = hidden_rows.astype(jnp.float32)
    inverse = lax.rsqrt(jnp.mean(widened * widened, axis=-1, keepdims=True) + 1e-06)
    return (widened * inverse * norm_gain).astype(jnp.bfloat16)


def dot(a, b):
    return jnp.dot(a, b, preferred_element_type=jnp.float32)


def spread(block, axis):
    size = math.prod(lax.axis_size(one) for one in (axis if isinstance(axis, tuple) else (axis,)))
    return lax.all_to_all(jnp.broadcast_to(block[None], (size,) + block.shape), axis, 0, 0, tiled=True)


def attend_sample(query, keys, values, step_keys, step_values, seen, chunk):
    scale = math.log2(math.e) / math.sqrt(HEAD_SIZE)
    contract = (((1,), (1,)), ((), ()))
    near = lax.dot_general(query, step_keys, contract, preferred_element_type=jnp.float32)
    near = jnp.where(seen, near, NEG_FILL)
    starts = range(0, keys.shape[0], chunk)
    far = [
        lax.dot_general(query, keys[at : at + chunk], contract, preferred_element_type=jnp.float32) for at in starts
    ]
    top = near.max(-1, keepdims=True)
    for scores in far:
        top = jnp.maximum(top, scores.max(-1, keepdims=True))
    top = top * scale
    weights = jnp.exp2(near * scale - top)
    total = weights.sum(-1, keepdims=True)
    attended = dot(weights.astype(jnp.bfloat16), step_values)
    for at, scores in zip(starts, far):
        weights = jnp.exp2(scores * scale - top)
        total = total + weights.sum(-1, keepdims=True)
        attended = attended + dot(weights.astype(jnp.bfloat16), values[at : at + chunk])
    return (attended / total).astype(jnp.bfloat16)


def attend_kernel(
    chunks, slots, normed, low_weights, high_weights, context, step_keyval, allowed, own_out, other_out, *scratch
):
    total, query, keys, values = scratch
    step = pl.program_id(0)
    heads = query.shape[1] // HEAD_SIZE
    depth = low_weights.shape[0]

    def unpack():
        count, quarter = context.shape[1], HEAD_SIZE // 2
        for hi in range(context.shape[0] // 4):
            for x in range(4):
                to, lane = (keys, values)[x // 2], x % 2 * quarter
                for side in range(2):
                    at = (hi * 2 + side) * count
                    to[at : at + count, lane : lane + quarter] = context[
                        hi * 4 + x, :, side * quarter : (side + 1) * quarter
                    ]

    for chunk in range(chunks):

        @pl.when(step == chunk)
        def _():
            low = normed[:, chunk * depth : (chunk + 1) * depth]
            high = normed[:, (chunks + chunk) * depth : (chunks + chunk + 1) * depth]
            both = dot(low, low_weights[...]) + dot(high, high_weights[...])
            if chunk == 0:
                total[...] = both
                unpack()
            else:
                total[...] += both

    @pl.when(step == chunks - 1)
    def _():
        query[...] = total[...].astype(jnp.bfloat16)

    def attend_rows(first, out):
        for at in range(0, out.shape[0], slots):
            here = slice(first + at, first + at + slots)
            own = query[here, :]
            own = jnp.concatenate([own[:, h * HEAD_SIZE : (h + 1) * HEAD_SIZE] for h in range(heads)], 0)
            seen = jnp.concatenate([allowed[here, :slots].astype(jnp.float32)] * heads, 0) > 0.5
            step_keys, step_values = step_keyval[here, :HEAD_SIZE], step_keyval[here, HEAD_SIZE:]
            result = attend_sample(own, keys, values, step_keys, step_values, seen, CHUNK)
            out[at : at + slots, :] = jnp.concatenate(
                [result[h * slots : (h + 1) * slots] for h in range(heads)], 1
            )

    @pl.when(step == chunks)
    def _():
        attend_rows(0, own_out)

    @pl.when(step == chunks + 1)
    def _():
        attend_rows(own_out.shape[0], other_out)


def attend(normed, query_weights, context, step_keyval, allowed, slots):
    rows, features = normed.shape
    half, cols = query_weights.shape[0], query_weights.shape[1] // 2
    tokens = context.shape[0] * context.shape[1] // 2
    chunks = half // DEPTH
    here = pl.BlockSpec(memory_space=pltpu.VMEM)
    return pl.pallas_call(
        functools.partial(attend_kernel, chunks, slots),
        grid=(chunks + 2,),
        in_specs=[
            here,
            pl.BlockSpec((DEPTH, cols), lambda i: (jnp.minimum(i, chunks - 1), 0)),
            pl.BlockSpec((DEPTH, cols), lambda i: (jnp.minimum(i, chunks - 1), 1)),
            here,
            pl.BlockSpec(step_keyval.shape, lambda i: (0, 0)),
            pl.BlockSpec(allowed.shape, lambda i: (0, 0)),
        ],
        out_specs=[here, here],
        out_shape=[jax.ShapeDtypeStruct((rows // 2, cols), jnp.bfloat16)] * 2,
        scratch_shapes=[pltpu.VMEM((rows, cols), jnp.float32), pltpu.VMEM((rows, cols), jnp.bfloat16)]
        + [pltpu.VMEM((tokens, HEAD_SIZE), jnp.bfloat16)] * 2,
        compiler_params=pltpu.CompilerParams(vmem_limit_bytes=50 * 2**20),
        cost_estimate=pl.CostEstimate(
            flops=4 * rows * cols * tokens + 2 * rows * cols * features,
            bytes_accessed=2 * features * cols,
            transcendentals=rows * tokens * cols // HEAD_SIZE,
        ),
    )(normed, query_weights, query_weights, context, step_keyval, allowed)


def project(rows, packed):
    features, width = rows.shape[1] // 2, packed.shape[1] // 2
    return dot(rows[:, :features], packed[:, :width]) + dot(rows[:, features:], packed[:, width:])


def pack(block):
    half = block.shape[-2] // 2
    return jnp.concatenate([block[..., :half, :], block[..., half:, :]], -1)


def local(ctx_hidden, step_hidden, norm_gain, w_query, w_keyval, step_lengths, step_mask):
    samples, slots, features = step_hidden.shape
    rows = samples * slots
    kv_heads = w_keyval.shape[1] // (2 * HEAD_SIZE)
    cols = w_query.shape[1] // kv_heads
    chips = lax.axis_size("x")
    quarter = 2 * HEAD_SIZE // chips
    core, x = lax.axis_index("core"), lax.axis_index("x")

    own_query = lax.dynamic_slice_in_dim(w_query, core * cols, cols, 1)
    start = (x // 2) * kv_heads * HEAD_SIZE + core * HEAD_SIZE + (x % 2) * quarter
    own_kv = lax.dynamic_slice_in_dim(w_keyval, start, quarter, 1)
    pair = lax.all_gather(jnp.concatenate([own_query, own_kv], 1), "yl", axis=0)
    pair_query = jnp.concatenate([pair[0, :, :cols], pair[1, :, :cols]], 1)
    pair_kv = jnp.concatenate([pair[0, :, cols:], pair[1, :, cols:]], 1)
    pair_query, pair_kv, step_hidden, ctx_hidden = lax.optimization_barrier(
        (pair_query, pair_kv, step_hidden, ctx_hidden)
    )
    query_weights = lax.all_gather(pair_query, "z", axis=0, tiled=True)
    yh = lax.axis_index("yh")
    rows_half = pair_kv.shape[0] // 2
    half_kv = spread(lax.dynamic_slice_in_dim(pair_kv, yh * rows_half, rows_half, 0), "z")
    rest_kv = lax.ppermute(half_kv, "yh", SWAP)
    low_first = yh == 0
    part_kv = jnp.concatenate([jnp.where(low_first, half_kv, rest_kv), jnp.where(low_first, rest_kv, half_kv)], 1)
    part_kv = part_kv.reshape(-1, 2 * quarter)

    own_tokens = ctx_hidden.shape[0] // 2
    own_context = lax.dynamic_slice_in_dim(ctx_hidden, yh * own_tokens, own_tokens, 0)
    context = project(rms_norm(own_context, norm_gain), part_kv).astype(jnp.bfloat16)
    context = lax.all_gather(pack(context), "yl", axis=0, tiled=True)
    part_kv = lax.optimization_barrier((part_kv, context))[0]
    context = spread(spread(context, "z").reshape(-1, 2 * quarter), ("yh", "x"))

    positions = lax.iota(jnp.int32, slots)
    causal = positions[None, :] <= positions[:, None]
    diagonal = positions[None, :] == positions[:, None]
    allowed = (
        causal[None]
        & (diagonal[None] | (step_mask == 1))
        & (positions[None, None, :] < step_lengths[:, None, None])
    )
    allowed = jnp.pad(allowed.astype(jnp.bfloat16).reshape(rows, slots), ((0, 0), (0, HEAD_SIZE - slots)))
    allowed = jnp.concatenate([allowed, lax.ppermute(allowed, "core", SWAP)], 0)
    normed_step = rms_norm(step_hidden.reshape(rows, features), norm_gain)
    both_rows = jnp.concatenate([normed_step, lax.ppermute(normed_step, "core", SWAP)], 0)

    turned = lambda block, turn: lax.ppermute(block, "x", [(i, (i - turn) % chips) for i in range(chips)])
    turns = [part_kv, turned(part_kv, 1)]
    late_kv = lax.optimization_barrier((part_kv, turns[1]))[0]
    turns += [turned(late_kv, turn) for turn in range(2, chips)]
    kv_weights = jnp.concatenate(
        [
            jnp.concatenate([one[:, :quarter] for one in turns], 1),
            jnp.concatenate([one[:, quarter:] for one in turns], 1),
        ],
        0,
    )
    step_keyval = dot(both_rows, kv_weights).astype(jnp.bfloat16)
    step_keyval = jnp.concatenate([step_keyval, step_keyval], 1)
    step_keyval = lax.dynamic_slice_in_dim(step_keyval, (chips - x) % chips * quarter, chips * quarter, 1)
    mine, theirs = attend(both_rows, query_weights, context, step_keyval, allowed, slots)

    theirs = lax.ppermute(theirs, "core", SWAP)
    live_rows = (positions[None, :] < step_lengths[:, None]).reshape(rows, 1)
    first = core == 0
    low = jnp.where(live_rows, jnp.where(first, mine, theirs), jnp.bfloat16(0.0))
    high = jnp.where(live_rows, jnp.where(first, theirs, mine), jnp.bfloat16(0.0))
    return jnp.concatenate([low, high], 1).reshape(samples, slots, kv_heads * cols)


def solution(mesh):
    five = Mesh(mesh.devices.reshape(2, 4, 2, 2, 16), AXES)
    dev, everywhere = ("yl", "z"), AXES
    placed = (
        P(dev, None),
        P(everywhere, None, None),
        P(),
        P(dev, None),
        P(dev, None),
        P(everywhere),
        P(everywhere, None, None),
    )
    return jax.shard_map(
        local, mesh=five, in_specs=placed, out_specs=P(everywhere, None, None), check_vma=False
    )
```

```python
import functools
import math

import jax
import jax.numpy as jnp
from jax import lax
from jax.experimental import pallas as pl
from jax.experimental.pallas import tpu as pltpu
from jax.sharding import Mesh
from jax.sharding import PartitionSpec as P

HEAD_SIZE = 128
NEG_FILL = -1e30
AXES = ("yh", "x", "core", "yl", "z")
SWAP = [(0, 1), (1, 0)]
CHUNK = 1024
DEPTH = 896


def rms_norm(hidden_rows, norm_gain):
    widened = hidden_rows.astype(jnp.float32)
    inverse = lax.rsqrt(jnp.mean(widened * widened, axis=-1, keepdims=True) + 1e-06)
    return (widened * inverse * norm_gain).astype(jnp.bfloat16)


def dot(a, b):
    return jnp.dot(a, b, preferred_element_type=jnp.float32)


def spread(block, axis):
    size = math.prod(lax.axis_size(one) for one in (axis if isinstance(axis, tuple) else (axis,)))
    return lax.all_to_all(jnp.broadcast_to(block[None], (size,) + block.shape), axis, 0, 0, tiled=True)


def attend_sample(query, keys, values, step_keys, step_values, seen, chunk):
    scale = math.log2(math.e) / math.sqrt(HEAD_SIZE)
    contract = (((1,), (1,)), ((), ()))
    near = lax.dot_general(query, step_keys, contract, preferred_element_type=jnp.float32)
    near = jnp.where(seen, near, NEG_FILL)
    starts = range(0, keys.shape[0], chunk)
    far = [
        lax.dot_general(query, keys[at : at + chunk], contract, preferred_element_type=jnp.float32) for at in starts
    ]
    top = near.max(-1, keepdims=True)
    for scores in far:
        top = jnp.maximum(top, scores.max(-1, keepdims=True))
    top = top * scale
    weights = jnp.exp2(near * scale - top)
    total = weights.sum(-1, keepdims=True)
    attended = dot(weights.astype(jnp.bfloat16), step_values)
    for at, scores in zip(starts, far):
        weights = jnp.exp2(scores * scale - top)
        total = total + weights.sum(-1, keepdims=True)
        attended = attended + dot(weights.astype(jnp.bfloat16), values[at : at + chunk])
    return (attended / total).astype(jnp.bfloat16)


def attend_kernel(
    chunks, slots, normed, low_weights, high_weights, context, step_keyval, allowed, own_out, other_out, *scratch
):
    total, query, keys, values = scratch
    step = pl.program_id(0)
    heads = query.shape[1] // HEAD_SIZE
    depth = low_weights.shape[0]

    def unpack():
        count, quarter = context.shape[1], HEAD_SIZE // 2
        for hi in range(context.shape[0] // 4):
            for x in range(4):
                to, lane = (keys, values)[x // 2], x % 2 * quarter
                for side in range(2):
                    at = (hi * 2 + side) * count
                    to[at : at + count, lane : lane + quarter] = context[
                        hi * 4 + x, :, side * quarter : (side + 1) * quarter
                    ]

    for chunk in range(chunks):

        @pl.when(step == chunk)
        def _():
            low = normed[:, chunk * depth : (chunk + 1) * depth]
            high = normed[:, (chunks + chunk) * depth : (chunks + chunk + 1) * depth]
            both = dot(low, low_weights[...]) + dot(high, high_weights[...])
            if chunk == 0:
                total[...] = both
                unpack()
            else:
                total[...] += both

    @pl.when(step == chunks - 1)
    def _():
        query[...] = total[...].astype(jnp.bfloat16)

    def attend_rows(first, out):
        for at in range(0, out.shape[0], slots):
            here = slice(first + at, first + at + slots)
            own = query[here, :]
            own = jnp.concatenate([own[:, h * HEAD_SIZE : (h + 1) * HEAD_SIZE] for h in range(heads)], 0)
            seen = jnp.concatenate([allowed[here, :slots].astype(jnp.float32)] * heads, 0) > 0.5
            step_keys, step_values = step_keyval[here, :HEAD_SIZE], step_keyval[here, HEAD_SIZE:]
            result = attend_sample(own, keys, values, step_keys, step_values, seen, CHUNK)
            out[at : at + slots, :] = jnp.concatenate(
                [result[h * slots : (h + 1) * slots] for h in range(heads)], 1
            )

    @pl.when(step == chunks)
    def _():
        attend_rows(0, own_out)

    @pl.when(step == chunks + 1)
    def _():
        attend_rows(own_out.shape[0], other_out)


def attend(normed, query_weights, context, step_keyval, allowed, slots):
    rows, features = normed.shape
    half, cols = query_weights.shape[0], query_weights.shape[1] // 2
    tokens = context.shape[0] * context.shape[1] // 2
    chunks = half // DEPTH
    here = pl.BlockSpec(memory_space=pltpu.VMEM)
    return pl.pallas_call(
        functools.partial(attend_kernel, chunks, slots),
        grid=(chunks + 2,),
        in_specs=[
            here,
            pl.BlockSpec((DEPTH, cols), lambda i: (jnp.minimum(i, chunks - 1), 0)),
            pl.BlockSpec((DEPTH, cols), lambda i: (jnp.minimum(i, chunks - 1), 1)),
            here,
            pl.BlockSpec(step_keyval.shape, lambda i: (0, 0)),
            pl.BlockSpec(allowed.shape, lambda i: (0, 0)),
        ],
        out_specs=[here, here],
        out_shape=[jax.ShapeDtypeStruct((rows // 2, cols), jnp.bfloat16)] * 2,
        scratch_shapes=[pltpu.VMEM((rows, cols), jnp.float32), pltpu.VMEM((rows, cols), jnp.bfloat16)]
        + [pltpu.VMEM((tokens, HEAD_SIZE), jnp.bfloat16)] * 2,
        compiler_params=pltpu.CompilerParams(vmem_limit_bytes=50 * 2**20),
        cost_estimate=pl.CostEstimate(
            flops=4 * rows * cols * tokens + 2 * rows * cols * features,
            bytes_accessed=2 * features * cols,
            transcendentals=rows * tokens * cols // HEAD_SIZE,
        ),
    )(normed, query_weights, query_weights, context, step_keyval, allowed)


def project(rows, packed):
    features, width = rows.shape[1] // 2, packed.shape[1] // 2
    return dot(rows[:, :features], packed[:, :width]) + dot(rows[:, features:], packed[:, width:])


def pack(block):
    half = block.shape[-2] // 2
    return jnp.concatenate([block[..., :half, :], block[..., half:, :]], -1)


def local(ctx_hidden, step_hidden, norm_gain, w_query, w_keyval, step_lengths, step_mask):
    samples, slots, features = step_hidden.shape
    rows = samples * slots
    kv_heads = w_keyval.shape[1] // (2 * HEAD_SIZE)
    cols = w_query.shape[1] // kv_heads
    chips = lax.axis_size("x")
    quarter = 2 * HEAD_SIZE // chips
    core, x = lax.axis_index("core"), lax.axis_index("x")

    own_query = lax.dynamic_slice_in_dim(w_query, core * cols, cols, 1)
    start = (x // 2) * kv_heads * HEAD_SIZE + core * HEAD_SIZE + (x % 2) * quarter
    own_kv = lax.dynamic_slice_in_dim(w_keyval, start, quarter, 1)
    pair = lax.all_gather(jnp.concatenate([own_query, own_kv], 1), "yl", axis=0)
    pair_query = jnp.concatenate([pair[0, :, :cols], pair[1, :, :cols]], 1)
    pair_kv = jnp.concatenate([pair[0, :, cols:], pair[1, :, cols:]], 1)
    pair_query, pair_kv, step_hidden, ctx_hidden = lax.optimization_barrier(
        (pair_query, pair_kv, step_hidden, ctx_hidden)
    )
    query_weights = lax.all_gather(pair_query, "z", axis=0, tiled=True)
    yh = lax.axis_index("yh")
    rows_half = pair_kv.shape[0] // 2
    half_kv = spread(lax.dynamic_slice_in_dim(pair_kv, yh * rows_half, rows_half, 0), "z")
    rest_kv = lax.ppermute(half_kv, "yh", SWAP)
    low_first = yh == 0
    part_kv = jnp.concatenate([jnp.where(low_first, half_kv, rest_kv), jnp.where(low_first, rest_kv, half_kv)], 1)
    part_kv = part_kv.reshape(-1, 2 * quarter)

    own_tokens = ctx_hidden.shape[0] // 2
    own_context = lax.dynamic_slice_in_dim(ctx_hidden, yh * own_tokens, own_tokens, 0)
    context = project(rms_norm(own_context, norm_gain), part_kv).astype(jnp.bfloat16)
    context = lax.all_gather(pack(context), "yl", axis=0, tiled=True)
    part_kv = lax.optimization_barrier((part_kv, context))[0]
    context = spread(spread(context, "z").reshape(-1, 2 * quarter), ("yh", "x"))

    positions = lax.iota(jnp.int32, slots)
    causal = positions[None, :] <= positions[:, None]
    diagonal = positions[None, :] == positions[:, None]
    allowed = (
        causal[None]
        & (diagonal[None] | (step_mask == 1))
        & (positions[None, None, :] < step_lengths[:, None, None])
    )
    allowed = jnp.pad(allowed.astype(jnp.bfloat16).reshape(rows, slots), ((0, 0), (0, HEAD_SIZE - slots)))
    allowed = jnp.concatenate([allowed, lax.ppermute(allowed, "core", SWAP)], 0)
    normed_step = rms_norm(step_hidden.reshape(rows, features), norm_gain)
    both_rows = jnp.concatenate([normed_step, lax.ppermute(normed_step, "core", SWAP)], 0)

    late_kv = lax.optimization_barrier((part_kv, both_rows))[0]
    turns = [part_kv] + [
        lax.ppermute(late_kv, "x", [(i, (i - turn) % chips) for i in range(chips)]) for turn in range(1, chips)
    ]
    kv_weights = jnp.concatenate(
        [
            jnp.concatenate([one[:, :quarter] for one in turns], 1),
            jnp.concatenate([one[:, quarter:] for one in turns], 1),
        ],
        0,
    )
    step_keyval = dot(both_rows, kv_weights).astype(jnp.bfloat16)
    step_keyval = jnp.concatenate([step_keyval, step_keyval], 1)
    step_keyval = lax.dynamic_slice_in_dim(step_keyval, (chips - x) % chips * quarter, chips * quarter, 1)
    mine, theirs = attend(both_rows, query_weights, context, step_keyval, allowed, slots)

    theirs = lax.ppermute(theirs, "core", SWAP)
    live_rows = (positions[None, :] < step_lengths[:, None]).reshape(rows, 1)
    first = core == 0
    low = jnp.where(live_rows, jnp.where(first, mine, theirs), jnp.bfloat16(0.0))
    high = jnp.where(live_rows, jnp.where(first, theirs, mine), jnp.bfloat16(0.0))
    return jnp.concatenate([low, high], 1).reshape(samples, slots, kv_heads * cols)


def solution(mesh):
    five = Mesh(mesh.devices.reshape(2, 4, 2, 2, 16), AXES)
    dev, everywhere = ("yl", "z"), AXES
    placed = (
        P(dev, None),
        P(everywhere, None, None),
        P(),
        P(dev, None),
        P(dev, None),
        P(everywhere),
        P(everywhere, None, None),
    )
    return jax.shard_map(
        local, mesh=five, in_specs=placed, out_specs=P(everywhere, None, None), check_vma=False
    )
```

```python
import functools
import math

import jax
import jax.numpy as jnp
from jax import lax
from jax.experimental import pallas as pl
from jax.experimental.pallas import tpu as pltpu
from jax.sharding import Mesh
from jax.sharding import PartitionSpec as P

HEAD_SIZE = 128
NEG_FILL = -1e30
AXES = ("yh", "x", "core", "yl", "z")
SWAP = [(0, 1), (1, 0)]
CHUNK = 1024
DEPTH = 896


def rms_norm(hidden_rows, norm_gain):
    widened = hidden_rows.astype(jnp.float32)
    inverse = lax.rsqrt(jnp.mean(widened * widened, axis=-1, keepdims=True) + 1e-06)
    return (widened * inverse * norm_gain).astype(jnp.bfloat16)


def dot(a, b):
    return jnp.dot(a, b, preferred_element_type=jnp.float32)


def spread(block, axis):
    size = math.prod(lax.axis_size(one) for one in (axis if isinstance(axis, tuple) else (axis,)))
    return lax.all_to_all(jnp.broadcast_to(block[None], (size,) + block.shape), axis, 0, 0, tiled=True)


def attend_sample(query, keys, values, step_keys, step_values, seen, chunk):
    scale = math.log2(math.e) / math.sqrt(HEAD_SIZE)
    contract = (((1,), (1,)), ((), ()))
    near = lax.dot_general(query, step_keys, contract, preferred_element_type=jnp.float32)
    near = jnp.where(seen, near, NEG_FILL)
    starts = range(0, keys.shape[0], chunk)
    far = [
        lax.dot_general(query, keys[at : at + chunk], contract, preferred_element_type=jnp.float32) for at in starts
    ]
    top = near.max(-1, keepdims=True)
    for scores in far:
        top = jnp.maximum(top, scores.max(-1, keepdims=True))
    top = top * scale
    weights = jnp.exp2(near * scale - top)
    total = weights.sum(-1, keepdims=True)
    attended = dot(weights.astype(jnp.bfloat16), step_values)
    for at, scores in zip(starts, far):
        weights = jnp.exp2(scores * scale - top)
        total = total + weights.sum(-1, keepdims=True)
        attended = attended + dot(weights.astype(jnp.bfloat16), values[at : at + chunk])
    return (attended * (1.0 / total)).astype(jnp.bfloat16)


def attend_kernel(
    chunks, slots, normed, low_weights, high_weights, context, step_keyval, allowed, own_out, other_out, *scratch
):
    total, query, keys, values = scratch
    step = pl.program_id(0)
    heads = query.shape[1] // HEAD_SIZE
    depth = low_weights.shape[0]

    def unpack():
        count, quarter = context.shape[1], HEAD_SIZE // 2
        for hi in range(context.shape[0] // 4):
            for x in range(4):
                to, lane = (keys, values)[x // 2], x % 2 * quarter
                for side in range(2):
                    at = (hi * 2 + side) * count
                    to[at : at + count, lane : lane + quarter] = context[
                        hi * 4 + x, :, side * quarter : (side + 1) * quarter
                    ]

    for chunk in range(chunks):

        @pl.when(step == chunk)
        def _():
            low = normed[:, chunk * depth : (chunk + 1) * depth]
            high = normed[:, (chunks + chunk) * depth : (chunks + chunk + 1) * depth]
            both = dot(low, low_weights[...]) + dot(high, high_weights[...])
            if chunk == 0:
                total[...] = both
                unpack()
            else:
                total[...] += both

    @pl.when(step == chunks - 1)
    def _():
        query[...] = total[...].astype(jnp.bfloat16)

    def attend_rows(first, out):
        for at in range(0, out.shape[0], slots):
            here = slice(first + at, first + at + slots)
            own = query[here, :]
            own = jnp.concatenate([own[:, h * HEAD_SIZE : (h + 1) * HEAD_SIZE] for h in range(heads)], 0)
            seen = jnp.concatenate([allowed[here, :slots].astype(jnp.float32)] * heads, 0) > 0.5
            step_keys, step_values = step_keyval[here, :HEAD_SIZE], step_keyval[here, HEAD_SIZE:]
            result = attend_sample(own, keys, values, step_keys, step_values, seen, CHUNK)
            out[at : at + slots, :] = jnp.concatenate(
                [result[h * slots : (h + 1) * slots] for h in range(heads)], 1
            )

    @pl.when(step == chunks)
    def _():
        attend_rows(0, own_out)

    @pl.when(step == chunks + 1)
    def _():
        attend_rows(own_out.shape[0], other_out)


def attend(normed, query_weights, context, step_keyval, allowed, slots):
    rows, features = normed.shape
    half, cols = query_weights.shape[0], query_weights.shape[1] // 2
    tokens = context.shape[0] * context.shape[1] // 2
    chunks = half // DEPTH
    here = pl.BlockSpec(memory_space=pltpu.VMEM)
    return pl.pallas_call(
        functools.partial(attend_kernel, chunks, slots),
        grid=(chunks + 2,),
        in_specs=[
            here,
            pl.BlockSpec((DEPTH, cols), lambda i: (jnp.minimum(i, chunks - 1), 0)),
            pl.BlockSpec((DEPTH, cols), lambda i: (jnp.minimum(i, chunks - 1), 1)),
            here,
            pl.BlockSpec(step_keyval.shape, lambda i: (0, 0)),
            pl.BlockSpec(allowed.shape, lambda i: (0, 0)),
        ],
        out_specs=[here, here],
        out_shape=[jax.ShapeDtypeStruct((rows // 2, cols), jnp.bfloat16)] * 2,
        scratch_shapes=[pltpu.VMEM((rows, cols), jnp.float32), pltpu.VMEM((rows, cols), jnp.bfloat16)]
        + [pltpu.VMEM((tokens, HEAD_SIZE), jnp.bfloat16)] * 2,
        compiler_params=pltpu.CompilerParams(vmem_limit_bytes=50 * 2**20),
        cost_estimate=pl.CostEstimate(
            flops=4 * rows * cols * tokens + 2 * rows * cols * features,
            bytes_accessed=2 * features * cols,
            transcendentals=rows * tokens * cols // HEAD_SIZE,
        ),
    )(normed, query_weights, query_weights, context, step_keyval, allowed)


def project(rows, packed):
    features, width = rows.shape[1] // 2, packed.shape[1] // 2
    return dot(rows[:, :features], packed[:, :width]) + dot(rows[:, features:], packed[:, width:])


def pack(block):
    half = block.shape[-2] // 2
    return jnp.concatenate([block[..., :half, :], block[..., half:, :]], -1)


def local(ctx_hidden, step_hidden, norm_gain, w_query, w_keyval, step_lengths, step_mask):
    samples, slots, features = step_hidden.shape
    rows = samples * slots
    kv_heads = w_keyval.shape[1] // (2 * HEAD_SIZE)
    cols = w_query.shape[1] // kv_heads
    chips = lax.axis_size("x")
    quarter = 2 * HEAD_SIZE // chips
    core, x = lax.axis_index("core"), lax.axis_index("x")

    own_query = lax.dynamic_slice_in_dim(w_query, core * cols, cols, 1)
    start = (x // 2) * kv_heads * HEAD_SIZE + core * HEAD_SIZE + (x % 2) * quarter
    own_kv = lax.dynamic_slice_in_dim(w_keyval, start, quarter, 1)
    pair = lax.all_gather(jnp.concatenate([own_query, own_kv], 1), "yl", axis=0)
    pair_query = jnp.concatenate([pair[0, :, :cols], pair[1, :, :cols]], 1)
    pair_kv = jnp.concatenate([pair[0, :, cols:], pair[1, :, cols:]], 1)
    pair_query, pair_kv, step_hidden, ctx_hidden = lax.optimization_barrier(
        (pair_query, pair_kv, step_hidden, ctx_hidden)
    )
    query_weights = lax.all_gather(pair_query, "z", axis=0, tiled=True)
    yh = lax.axis_index("yh")
    rows_half = pair_kv.shape[0] // 2
    half_kv = spread(lax.dynamic_slice_in_dim(pair_kv, yh * rows_half, rows_half, 0), "z")
    rest_kv = lax.ppermute(half_kv, "yh", SWAP)
    low_first = yh == 0
    part_kv = jnp.concatenate([jnp.where(low_first, half_kv, rest_kv), jnp.where(low_first, rest_kv, half_kv)], 1)
    part_kv = part_kv.reshape(-1, 2 * quarter)

    own_tokens = ctx_hidden.shape[0] // 2
    own_context = lax.dynamic_slice_in_dim(ctx_hidden, yh * own_tokens, own_tokens, 0)
    context = project(rms_norm(own_context, norm_gain), part_kv).astype(jnp.bfloat16)
    context = lax.all_gather(pack(context), "yl", axis=0, tiled=True)
    part_kv = lax.optimization_barrier((part_kv, context))[0]
    context = spread(spread(context, "z").reshape(-1, 2 * quarter), ("yh", "x"))

    positions = lax.iota(jnp.int32, slots)
    causal = positions[None, :] <= positions[:, None]
    diagonal = positions[None, :] == positions[:, None]
    allowed = (
        causal[None]
        & (diagonal[None] | (step_mask == 1))
        & (positions[None, None, :] < step_lengths[:, None, None])
    )
    allowed = jnp.pad(allowed.astype(jnp.bfloat16).reshape(rows, slots), ((0, 0), (0, HEAD_SIZE - slots)))
    allowed = jnp.concatenate([allowed, lax.ppermute(allowed, "core", SWAP)], 0)
    normed_step = rms_norm(step_hidden.reshape(rows, features), norm_gain)
    both_rows = jnp.concatenate([normed_step, lax.ppermute(normed_step, "core", SWAP)], 0)

    late_kv = lax.optimization_barrier((part_kv, both_rows))[0]
    turns = [part_kv] + [
        lax.ppermute(late_kv, "x", [(i, (i - turn) % chips) for i in range(chips)]) for turn in range(1, chips)
    ]
    kv_weights = jnp.concatenate(
        [
            jnp.concatenate([one[:, :quarter] for one in turns], 1),
            jnp.concatenate([one[:, quarter:] for one in turns], 1),
        ],
        0,
    )
    step_keyval = dot(both_rows, kv_weights).astype(jnp.bfloat16)
    step_keyval = jnp.concatenate([step_keyval, step_keyval], 1)
    step_keyval = lax.dynamic_slice_in_dim(step_keyval, (chips - x) % chips * quarter, chips * quarter, 1)
    mine, theirs = attend(both_rows, query_weights, context, step_keyval, allowed, slots)

    theirs = lax.ppermute(theirs, "core", SWAP)
    live_rows = (positions[None, :] < step_lengths[:, None]).reshape(rows, 1)
    first = core == 0
    low = jnp.where(live_rows, jnp.where(first, mine, theirs), jnp.bfloat16(0.0))
    high = jnp.where(live_rows, jnp.where(first, theirs, mine), jnp.bfloat16(0.0))
    return jnp.concatenate([low, high], 1).reshape(samples, slots, kv_heads * cols)


def solution(mesh):
    five = Mesh(mesh.devices.reshape(2, 4, 2, 2, 16), AXES)
    dev, everywhere = ("yl", "z"), AXES
    placed = (
        P(dev, None),
        P(everywhere, None, None),
        P(),
        P(dev, None),
        P(dev, None),
        P(everywhere),
        P(everywhere, None, None),
    )
    return jax.shard_map(
        local, mesh=five, in_specs=placed, out_specs=P(everywhere, None, None), check_vma=False
    )
```
